32 devices in a mesh: blk: 4 (over y, x), wide: 8 (over z, core).
Axes of the slice: x: 2, y: 2, z: 4, core: 2. Of those that a mesh axis runs over, the one named last changes fastest.
Arguments:
- a_blocks: float32 [16, 4, 8, 4, 128, 128], P('blk', None, 'wide'), may hold values from -6 to 6
- a_map: int32 [16, 4, 8, 4], P('blk', None, 'wide'), may hold values 0 or 1
- b_blocks: float32 [4, 8, 4, 8, 128, 128], P('blk', 'wide'), may hold values from -0.09375 to 0.09375
- b_map: int32 [4, 8, 4, 8], P('blk', 'wide'), may hold values 0 or 1
- owner_map: int32 [16, 8], P('blk'), may hold values from -1 to 7, as said below
Outputs:
- owned: float32 [4, 8, 8, 128, 128], P('blk', 'wide')
The draws below stay inside these ranges and needn't reach their ends.
Inputs may be any that keep to these rules, and one draw needn't show every extreme that they name: `owner_map`: in each panel of 4 x 8 product blocks (block rows i * 4 to i * 4 + 3), each owner holds at most 8 blocks, and one owner holds exactly 8.
All inputs are finite; a program needn't handle non-finite values. No bound on the sum of `a_map` or of `b_map` on one device may be relied on, other than what follows from the above.
Results may differ from the reference program's by a relative error of at most 0.00007.
Values sent between devices are 32-bit elements; how exact they have to be, the bound alone decides.
A program may use at most 128 MiB of HBM per device.

```python
import jax
import jax.numpy as jnp
from jax import lax

BS = 128
KBD = 4
RB = 4
CBT = 8
NRB = 16
ORDER = 16384
CAP = 8
N_BLK = 4
N_WIDE = 8


def draw_owner_map(key, part):
    panel_size = RB * CBT
    pool_size = (N_WIDE - 1) * CAP + panel_size // 4

    def one_panel(panel_key):
        first_key, second_key, third_key = jax.random.split(panel_key, 3)
        busiest = jax.random.randint(first_key, (), 0, N_WIDE, dtype=jnp.int32)
        places = jnp.arange(pool_size, dtype=jnp.int32)
        others = (busiest + 1 + places // CAP) % N_WIDE
        pool = jnp.where(places < (N_WIDE - 1) * CAP, others, -1).astype(jnp.int32)
        pool = jax.random.permutation(second_key, pool)
        listed = jnp.concatenate([jnp.zeros((CAP,), jnp.int32) + busiest, pool[:panel_size - CAP]])
        listed = jax.random.permutation(third_key, listed)
        return listed.reshape(RB, CBT)
    panel_keys = jax.random.split(jax.random.fold_in(key, 17), N_BLK)
    return jax.vmap(one_panel)(panel_keys).reshape(N_BLK * RB, CBT).astype(jnp.int32)


def plant(array, own_key, low, largest):
    extent = array.shape
    spot = [jax.random.randint(jax.random.fold_in(own_key, axis), (), 0, extent[axis]) for axis in range(len(extent))]
    array = array.at[tuple(spot)].set(low)
    longest = extent.index(max(extent))
    spot[longest] = (spot[longest] + 1) % extent[longest]
    return array.at[tuple(spot)].set(largest)


def block_scale(key, shape, pieces, least, high):
    def one(axis_at, parts):
        draws = jax.random.uniform(jax.random.fold_in(jax.random.fold_in(key, 6), axis_at), (parts,), jnp.float32, least / len(pieces), high / len(pieces))
        return jnp.repeat(jnp.exp(draws), shape[axis_at] // parts).reshape((-1,) + (1,) * (len(shape) - axis_at - 1))

    level = one(*pieces[0])
    for cut in pieces[1:]:
        level = level * one(*cut)
    return level


def scatter_about(own_key, dims, spread, most, shards=(), kind=jnp.bfloat16):
    loudness = block_scale(own_key, dims, shards, -0.22, 0.18) if shards else 1.0
    array = jax.random.normal(own_key, dims, jnp.float32) * spread * loudness
    return jnp.minimum(jnp.maximum(array, -most), most).astype(kind)


def setup_inputs(seed: int = 0) -> dict:
    seeds = jax.random.split(jax.random.key(seed), 6)
    return {
        "a_blocks": scatter_about(seeds[0], (NRB, N_BLK, N_WIDE, KBD, BS, BS), 1.0, 6.0, ((0, 4), (2, 8)), jnp.float32),
        "a_map": plant((jax.random.randint(seeds[1], (NRB, N_BLK, N_WIDE, KBD), 0, 2) < 1).astype(jnp.int32), jax.random.fold_in(seeds[1], 1), 0, 1),
        "b_blocks": scatter_about(seeds[2], (N_BLK, N_WIDE, KBD, CBT, BS, BS), (ORDER // 4) ** -0.5, 0.09375, ((0, 4), (1, 8)), jnp.float32),
        "b_map": plant((jax.random.randint(seeds[3], (N_BLK, N_WIDE, KBD, CBT), 0, 2) < 1).astype(jnp.int32), jax.random.fold_in(seeds[3], 1), 0, 1),
        "owner_map": draw_owner_map(jax.random.fold_in(seeds[5], 71), 0),
    }


def reference(a_blocks, a_map, b_blocks, b_map, owner_map):
    highest = lax.Precision.HIGHEST
    right_used = b_blocks * b_map[..., None, None].astype(b_blocks.dtype)

    def one_row(row_pair):
        block_row, row_mask = row_pair
        left_used = block_row * row_mask[..., None, None].astype(block_row.dtype)
        return jnp.einsum("jwtxy,jwtcyz->cxz", left_used, right_used, precision=highest)

    product = lax.map(one_row, (a_blocks, a_map))
    groups = product.reshape(N_BLK, RB * CBT, BS, BS)
    owner_list = owner_map.reshape(N_BLK, RB * CBT)
    owner_hit = (owner_list[:, :, None] == jnp.arange(N_WIDE, dtype=jnp.int32)[None, None, :]).astype(jnp.int32)
    slot_rank = jnp.cumsum(owner_hit, axis=1) - owner_hit
    slot_match = (slot_rank[..., None] == jnp.arange(CAP, dtype=jnp.int32)).astype(jnp.int32)
    selector = (owner_hit[..., None] * slot_match).astype(product.dtype)
    return jnp.einsum("iqos,iqxy->iosxy", selector, groups, precision=highest)
```

```python
import functools

import jax
import jax.numpy as jnp
from jax import lax
from jax.experimental import pallas as pl
from jax.experimental.pallas import tpu as pltpu
from jax.sharding import PartitionSpec as P

MESH = pl.DeviceIdType.MESH
AHEAD = 2


def ring_place(index, n):
    half = n // 2
    return jnp.where(index < half, index, n + half - 1 - index)


def kernel(
    n, wide, amap_ref, bmap_ref, owner_ref, a_ref, b_ref, out_ref,
    a_raw, a_hi, a_lo, gathered, partial_c, half_in, half_sum, piece_in, panel,
    a_sem, g_send, g_recv, x_send, x_recv, z_send, z_recv, p_send, p_recv, s_send, s_recv,
):
    rows, _, _, inner, side, _ = a_ref.shape
    chunks = b_ref.shape[3]
    hops = n // 2
    mates = wide // 2
    chunk_rows = rows * side
    half_rows = chunk_rows // 2
    piece = chunk_rows // wide

    blk, me = lax.axis_index("blk"), lax.axis_index("wide")
    place = ring_place(blk, n)
    right = ring_place(lax.rem(place + 1, n), n)
    left = ring_place(lax.rem(place + n - 1, n), n)
    core, chip = lax.rem(me, 2), me // 2
    partner = me + 1 - 2 * core
    mate = [None] + [2 * lax.rem(chip + d, mates) + core for d in range(1, mates)]
    my_half = pl.multiple_of(core * half_rows, 8)
    other_half = pl.multiple_of((1 - core) * half_rows, 8)
    my_place = core * half_rows + chip * piece
    my_row, my_start = my_place // side, pl.multiple_of(lax.rem(my_place, side), 8)

    load_a = pltpu.make_async_copy(a_ref, a_raw, a_sem)
    load_a.start()

    barrier = pltpu.get_barrier_semaphore()
    for other in (left, right):
        pl.semaphore_signal(barrier, inc=1, device_id=(other, me), device_id_type=MESH)
    for other in [partner] + mate[1:]:
        pl.semaphore_signal(barrier, inc=1, device_id=(blk, other), device_id_type=MESH)

    @pl.loop(0, chunks)
    def _(k):
        for t in range(inner):
            gathered[0, k, t] = b_ref[0, 0, t, k] * bmap_ref[0, 0, t, k].astype(jnp.float32)

    pl.semaphore_wait(barrier, 2 + mates)

    def hop(k, s, way):
        src = s - 1 if way == 0 else (n - s + 1) % n
        dst = s if way == 0 else n - s
        part = pl.ds(0, inner)
        if s == hops:
            part = pl.ds(0, inner // 2) if way == 0 else pl.ds(inner // 2, inner - inner // 2)
        return pltpu.make_async_remote_copy(
            src_ref=gathered.at[src, k, part],
            dst_ref=gathered.at[dst, k, part],
            send_sem=g_send.at[way, k, s - 1],
            recv_sem=g_recv.at[way, k, s - 1],
            device_id=(right if way == 0 else left, me),
            device_id_type=MESH,
        )

    def start_hop(k, s):
        for way in (0, 1):
            hop(k, s, way).start()

    def cross(k):
        return pltpu.make_async_remote_copy(
            src_ref=partial_c.at[k, pl.ds(other_half, half_rows)],
            dst_ref=half_in.at[k],
            send_sem=x_send.at[k],
            recv_sem=x_recv.at[k],
            device_id=(blk, partner),
            device_id_type=MESH,
        )

    def scatter(k, d):
        to = pl.multiple_of(lax.rem(chip + d, mates) * piece, 8)
        return pltpu.make_async_remote_copy(
            src_ref=half_sum.at[k, pl.ds(to, piece)],
            dst_ref=piece_in.at[k, d - 1],
            send_sem=z_send.at[k],
            recv_sem=z_recv.at[k],
            device_id=(blk, mate[d]),
            device_id_type=MESH,
        )

    def spread(k, d):
        return pltpu.make_async_remote_copy(
            src_ref=panel.at[k * rows + my_row, pl.ds(my_start, piece)],
            dst_ref=panel.at[k * rows + my_row, pl.ds(my_start, piece)],
            send_sem=p_send.at[k],
            recv_sem=p_recv.at[k],
            device_id=(blk, mate[d]),
            device_id_type=MESH,
        )

    def share(k):
        return pltpu.make_async_remote_copy(
            src_ref=panel.at[pl.ds(k * rows + core * (rows // 2), rows // 2)],
            dst_ref=panel.at[pl.ds(k * rows + core * (rows // 2), rows // 2)],
            send_sem=s_send.at[k],
            recv_sem=s_recv.at[k],
            device_id=(blk, partner),
            device_id_type=MESH,
        )

    def wait_pieces(k, sem):
        pltpu.make_async_copy(piece_in.at[k], piece_in.at[k], sem.at[k]).wait()

    def compute(k):
        partial_c[k] = jnp.zeros((chunk_rows, side), jnp.float32)

        @pl.loop(0, n)
        def _(d):
            right_part = gathered[d, k].reshape(inner * side, side)
            high = right_part.astype(jnp.bfloat16)
            low = (right_part - high.astype(jnp.float32)).astype(jnp.bfloat16)
            both = jnp.dot(
                a_hi[d], jnp.concatenate([high, low], axis=1), preferred_element_type=jnp.float32
            )
            rest = jnp.dot(a_lo[d], high, preferred_element_type=jnp.float32)
            partial_c[k] += both[:, :side] + (both[:, side:] + rest)

    for k in range(min(AHEAD, chunks)):
        start_hop(k, 1)

    load_a.wait()

    @pl.loop(0, n)
    def _(d):
        origin = ring_place(lax.rem(place + n - d, n), n)
        for r in range(rows):
            for t in range(inner):
                block = a_raw[r, origin, 0, t] * amap_ref[r, origin, 0, t].astype(jnp.float32)
                high = block.astype(jnp.bfloat16)
                at = (d, pl.ds(r * side, side), pl.ds(t * side, side))
                a_hi[at] = high
                a_lo[at] = (block - high.astype(jnp.float32)).astype(jnp.bfloat16)

    here = lambda k: 0 <= k < chunks
    for turn in range(chunks + hops - 1 + 4):
        for s in range(1, hops + 1):
            k = turn - (s - 1)
            if here(k):
                for way in (0, 1):
                    hop(k, s, way).wait_recv()
                if s < hops:
                    start_hop(k, s + 1)
            if s == 1 and here(k + AHEAD):
                start_hop(k + AHEAD, 1)
        k = turn - (hops - 1)
        if here(k):
            compute(k)
            cross(k).start()
        k -= 1
        if here(k):
            cross(k).wait_recv()
            half_sum[k] = partial_c[k, pl.ds(my_half, half_rows)] + half_in[k]
            for d in range(1, mates):
                scatter(k, d).start()
        k -= 1
        if here(k):
            wait_pieces(k, z_recv)
            total = half_sum[k, pl.ds(pl.multiple_of(chip * piece, 8), piece)]
            for d in range(1, mates):
                total = total + piece_in[k, d - 1]
            panel[k * rows + my_row, pl.ds(my_start, piece)] = total
            for d in range(1, mates):
                spread(k, d).start()
        k -= 1
        if here(k):
            wait_pieces(k, p_recv)
            share(k).start()

    slots = out_ref.shape[2]
    count = jnp.int32(0)
    found = [jnp.int32(-1)] * slots
    for q in range(rows * chunks):
        mine = owner_ref[q // chunks, q % chunks] == me
        at = (q % chunks) * rows + q // chunks
        found = [jnp.where(mine & (count == s), at, f) for s, f in enumerate(found)]
        count = count + mine.astype(jnp.int32)

    for k in range(chunks):
        share(k).wait_recv()
    for s in range(slots):
        taken = (found[s] >= 0).astype(jnp.float32)
        out_ref[0, 0, s] = panel[jnp.maximum(found[s], 0)] * taken

    for k in range(chunks):
        for s in range(1, hops + 1):
            for way in (0, 1):
                hop(k, s, way).wait_send()
        cross(k).wait_send()
        wait_pieces(k, z_send)
        wait_pieces(k, p_send)
        share(k).wait_send()


def per_device(n, wide, a_blocks, a_map, b_blocks, b_map, owner_map):
    rows, _, _, inner, side, _ = a_blocks.shape
    chunks = b_blocks.shape[3]
    hops, mates = n // 2, wide // 2
    chunk_rows = rows * side
    slots = max(2, 2 * rows * chunks // wide)
    f32, bf16 = jnp.float32, jnp.bfloat16
    dma = pltpu.SemaphoreType.DMA
    flops = 3 * 2 * chunk_rows * n * inner * side * chunks * side
    return pl.pallas_call(
        functools.partial(kernel, n, wide),
        out_shape=jax.ShapeDtypeStruct((1, 1, slots, side, side), f32),
        in_specs=[pl.BlockSpec(memory_space=pltpu.SMEM)] * 3
        + [pl.BlockSpec(memory_space=pl.ANY), pl.BlockSpec(memory_space=pltpu.VMEM)],
        out_specs=pl.BlockSpec(memory_space=pltpu.VMEM),
        scratch_shapes=[
            pltpu.VMEM(a_blocks.shape, f32),
            pltpu.VMEM((n, chunk_rows, inner * side), bf16),
            pltpu.VMEM((n, chunk_rows, inner * side), bf16),
            pltpu.VMEM((n, chunks, inner, side, side), f32),
            pltpu.VMEM((chunks, chunk_rows, side), f32),
            pltpu.VMEM((chunks, chunk_rows // 2, side), f32),
            pltpu.VMEM((chunks, chunk_rows // 2, side), f32),
            pltpu.VMEM((chunks, mates - 1, chunk_rows // wide, side), f32),
            pltpu.VMEM((chunks * rows, side, side), f32),
            dma,
            dma((2, chunks, hops)),
            dma((2, chunks, hops)),
        ]
        + [dma((chunks,))] * 8,
        compiler_params=pltpu.CompilerParams(
            collective_id=0, has_side_effects=True, vmem_limit_bytes=56 * 2**20
        ),
        cost_estimate=pl.CostEstimate(
            flops=flops, bytes_accessed=8 * 2**20, transcendentals=0
        ),
    )(a_map, b_map, owner_map, a_blocks, b_blocks)


def solution(mesh):
    in_specs = (
        P("blk", None, "wide", None, None, None),
        P("blk", None, "wide", None),
        P("blk", "wide", None, None, None, None),
        P("blk", "wide", None, None),
        P("blk", None),
    )
    out_specs = P("blk", "wide", None, None, None)
    return jax.shard_map(
        functools.partial(per_device, mesh.shape["blk"], mesh.shape["wide"]),
        mesh=mesh, in_specs=in_specs, out_specs=out_specs, check_vma=False,
    )
```

```python
import functools

import jax
import jax.numpy as jnp
from jax import lax
from jax.experimental import pallas as pl
from jax.experimental.pallas import tpu as pltpu
from jax.sharding import PartitionSpec as P

MESH = pl.DeviceIdType.MESH
AHEAD = 2


def ring_place(index, n):
    half = n // 2
    return jnp.where(index < half, index, n + half - 1 - index)


def kernel(
    n, wide, amap_ref, bmap_ref, owner_ref, a_ref, b_ref, out_ref,
    a_raw, b_raw, a_hi, a_lo, gathered, partial_c, half_in, half_sum, piece_in, panel,
    a_sem, b_sem, g_send, g_recv, x_send, x_recv, z_send, z_recv, p_send, p_recv, s_send, s_recv,
):
    rows, _, _, inner, side, _ = a_ref.shape
    chunks = b_ref.shape[3]
    hops = n // 2
    mates = wide // 2
    chunk_rows = rows * side
    half_rows = chunk_rows // 2
    piece = chunk_rows // wide

    blk, me = lax.axis_index("blk"), lax.axis_index("wide")
    place = ring_place(blk, n)
    right = ring_place(lax.rem(place + 1, n), n)
    left = ring_place(lax.rem(place + n - 1, n), n)
    core, chip = lax.rem(me, 2), me // 2
    partner = me + 1 - 2 * core
    mate = [None] + [2 * lax.rem(chip + d, mates) + core for d in range(1, mates)]
    my_half = pl.multiple_of(core * half_rows, 8)
    other_half = pl.multiple_of((1 - core) * half_rows, 8)
    my_place = core * half_rows + chip * piece
    my_row, my_start = my_place // side, pl.multiple_of(lax.rem(my_place, side), 8)

    def load_b(k):
        return pltpu.make_async_copy(b_ref.at[0, 0, :, k], b_raw.at[k], b_sem.at[k])

    load_a = pltpu.make_async_copy(a_ref, a_raw, a_sem)
    for k in range(chunks):
        load_b(k).start()
    load_a.start()

    barrier = pltpu.get_barrier_semaphore()
    for other in (left, right):
        pl.semaphore_signal(barrier, inc=1, device_id=(other, me), device_id_type=MESH)
    for other in [partner] + mate[1:]:
        pl.semaphore_signal(barrier, inc=1, device_id=(blk, other), device_id_type=MESH)

    def mask_b(k):
        load_b(k).wait()
        for t in range(inner):
            gathered[0, k, t] = b_raw[k, t] * bmap_ref[0, 0, t, k].astype(jnp.float32)

    mask_b(0)
    pl.semaphore_wait(barrier, 2 + mates)

    def hop(k, s, way):
        src = s - 1 if way == 0 else (n - s + 1) % n
        dst = s if way == 0 else n - s
        part = pl.ds(0, inner)
        if s == hops:
            part = pl.ds(0, inner // 2) if way == 0 else pl.ds(inner // 2, inner - inner // 2)
        return pltpu.make_async_remote_copy(
            src_ref=gathered.at[src, k, part],
            dst_ref=gathered.at[dst, k, part],
            send_sem=g_send.at[way, k, s - 1],
            recv_sem=g_recv.at[way, k, s - 1],
            device_id=(right if way == 0 else left, me),
            device_id_type=MESH,
        )

    def start_hop(k, s):
        for way in (0, 1):
            hop(k, s, way).start()

    def cross(k):
        return pltpu.make_async_remote_copy(
            src_ref=partial_c.at[k, pl.ds(other_half, half_rows)],
            dst_ref=half_in.at[k],
            send_sem=x_send.at[k],
            recv_sem=x_recv.at[k],
            device_id=(blk, partner),
            device_id_type=MESH,
        )

    def scatter(k, d):
        to = pl.multiple_of(lax.rem(chip + d, mates) * piece, 8)
        return pltpu.make_async_remote_copy(
            src_ref=half_sum.at[k, pl.ds(to, piece)],
            dst_ref=piece_in.at[k, d - 1],
            send_sem=z_send.at[k],
            recv_sem=z_recv.at[k],
            device_id=(blk, mate[d]),
            device_id_type=MESH,
        )

    def spread(k, d):
        return pltpu.make_async_remote_copy(
            src_ref=panel.at[k * rows + my_row, pl.ds(my_start, piece)],
            dst_ref=panel.at[k * rows + my_row, pl.ds(my_start, piece)],
            send_sem=p_send.at[k],
            recv_sem=p_recv.at[k],
            device_id=(blk, mate[d]),
            device_id_type=MESH,
        )

    def share(k):
        return pltpu.make_async_remote_copy(
            src_ref=panel.at[pl.ds(k * rows + core * (rows // 2), rows // 2)],
            dst_ref=panel.at[pl.ds(k * rows + core * (rows // 2), rows // 2)],
            send_sem=s_send.at[k],
            recv_sem=s_recv.at[k],
            device_id=(blk, partner),
            device_id_type=MESH,
        )

    def wait_pieces(k, sem):
        pltpu.make_async_copy(piece_in.at[k], piece_in.at[k], sem.at[k]).wait()

    def add_slot(k, d, base):
        right_part = gathered[d, k].reshape(inner * side, side)
        high = right_part.astype(jnp.bfloat16)
        low = (right_part - high.astype(jnp.float32)).astype(jnp.bfloat16)
        both = jnp.dot(
            a_hi[d], jnp.concatenate([high, low], axis=1), preferred_element_type=jnp.float32
        )
        rest = jnp.dot(a_lo[d], high, preferred_element_type=jnp.float32)
        partial_c[k] = base + (both[:, :side] + (both[:, side:] + rest))

    def compute(k, s):
        if s == 1:
            partial_c[k] = jnp.zeros((chunk_rows, side), jnp.float32)
        if s == hops:
            add_slot(k, hops, partial_c[k])
            return
        first, stride, many = (n - 1, 1, 3) if s == 1 else (s, n - 2 * s, 2)

        @pl.loop(0, many)
        def _(i):
            add_slot(k, lax.rem(first + i * stride, n), partial_c[k])

    for k in range(min(AHEAD, chunks)):
        if k:
            mask_b(k)
        start_hop(k, 1)

    load_a.wait()

    @pl.loop(0, n)
    def _(d):
        origin = ring_place(lax.rem(place + n - d, n), n)
        for r in range(rows):
            for t in range(inner):
                block = a_raw[r, origin, 0, t] * amap_ref[r, origin, 0, t].astype(jnp.float32)
                high = block.astype(jnp.bfloat16)
                at = (d, pl.ds(r * side, side), pl.ds(t * side, side))
                a_hi[at] = high
                a_lo[at] = (block - high.astype(jnp.float32)).astype(jnp.bfloat16)

    here = lambda k: 0 <= k < chunks
    for turn in range(chunks + hops + 1):
        for s in range(1, hops):
            k = turn - (s - 1)
            if here(k):
                for way in (0, 1):
                    hop(k, s, way).wait_recv()
                start_hop(k, s + 1)
            if s == 1 and here(k + AHEAD):
                mask_b(k + AHEAD)
                start_hop(k + AHEAD, 1)
            if here(k):
                compute(k, s)
        k = turn - hops
        if here(k):
            wait_pieces(k, z_recv)
            total = half_sum[k, pl.ds(pl.multiple_of(chip * piece, 8), piece)]
            for d in range(1, mates):
                total = total + piece_in[k, d - 1]
            panel[k * rows + my_row, pl.ds(my_start, piece)] = total
            for d in range(1, mates):
                spread(k, d).start()
        k = turn - (hops - 1)
        if here(k):
            for way in (0, 1):
                hop(k, hops, way).wait_recv()
            compute(k, hops)
            cross(k).start()
            cross(k).wait_recv()
            half_sum[k] = partial_c[k, pl.ds(my_half, half_rows)] + half_in[k]
            for d in range(1, mates):
                scatter(k, d).start()
        k = turn - (hops + 1)
        if here(k):
            wait_pieces(k, p_recv)
            share(k).start()

    slots = out_ref.shape[2]
    count = jnp.int32(0)
    found = [jnp.int32(-1)] * slots
    for q in range(rows * chunks):
        mine = owner_ref[q // chunks, q % chunks] == me
        at = (q % chunks) * rows + q // chunks
        found = [jnp.where(mine & (count == s), at, f) for s, f in enumerate(found)]
        count = count + mine.astype(jnp.int32)

    for k in range(chunks):
        share(k).wait_recv()
    for s in range(slots):
        taken = (found[s] >= 0).astype(jnp.float32)
        out_ref[0, 0, s] = panel[jnp.maximum(found[s], 0)] * taken

    for k in range(chunks):
        for s in range(1, hops + 1):
            for way in (0, 1):
                hop(k, s, way).wait_send()
        cross(k).wait_send()
        wait_pieces(k, z_send)
        wait_pieces(k, p_send)
        share(k).wait_send()


def per_device(n, wide, a_blocks, a_map, b_blocks, b_map, owner_map):
    rows, _, _, inner, side, _ = a_blocks.shape
    chunks = b_blocks.shape[3]
    hops, mates = n // 2, wide // 2
    chunk_rows = rows * side
    slots = max(2, 2 * rows * chunks // wide)
    f32, bf16 = jnp.float32, jnp.bfloat16
    dma = pltpu.SemaphoreType.DMA
    flops = 3 * 2 * chunk_rows * n * inner * side * chunks * side
    return pl.pallas_call(
        functools.partial(kernel, n, wide),
        out_shape=jax.ShapeDtypeStruct((1, 1, slots, side, side), f32),
        in_specs=[pl.BlockSpec(memory_space=pltpu.SMEM)] * 3
        + [pl.BlockSpec(memory_space=pl.ANY)] * 2,
        out_specs=pl.BlockSpec(memory_space=pltpu.VMEM),
        scratch_shapes=[
            pltpu.VMEM(a_blocks.shape, f32),
            pltpu.VMEM((chunks, inner, side, side), f32),
            pltpu.VMEM((n, chunk_rows, inner * side), bf16),
            pltpu.VMEM((n, chunk_rows, inner * side), bf16),
            pltpu.VMEM((n, chunks, inner, side, side), f32),
            pltpu.VMEM((chunks, chunk_rows, side), f32),
            pltpu.VMEM((chunks, chunk_rows // 2, side), f32),
            pltpu.VMEM((chunks, chunk_rows // 2, side), f32),
            pltpu.VMEM((chunks, mates - 1, chunk_rows // wide, side), f32),
            pltpu.VMEM((chunks * rows, side, side), f32),
            dma,
            dma((chunks,)),
            dma((2, chunks, hops)),
            dma((2, chunks, hops)),
        ]
        + [dma((chunks,))] * 8,
        compiler_params=pltpu.CompilerParams(
            collective_id=0, has_side_effects=True, vmem_limit_bytes=56 * 2**20
        ),
        cost_estimate=pl.CostEstimate(
            flops=flops, bytes_accessed=8 * 2**20, transcendentals=0
        ),
    )(a_map, b_map, owner_map, a_blocks, b_blocks)


def solution(mesh):
    in_specs = (
        P("blk", None, "wide", None, None, None),
        P("blk", None, "wide", None),
        P("blk", "wide", None, None, None, None),
        P("blk", "wide", None, None),
        P("blk", None),
    )
    out_specs = P("blk", "wide", None, None, None)
    return jax.shard_map(
        functools.partial(per_device, mesh.shape["blk"], mesh.shape["wide"]),
        mesh=mesh, in_specs=in_specs, out_specs=out_specs, check_vma=False,
    )
```

```python
import functools

import jax
import jax.numpy as jnp
from jax import lax
from jax.experimental import pallas as pl
from jax.experimental.pallas import tpu as pltpu
from jax.sharding import PartitionSpec as P

MESH = pl.DeviceIdType.MESH
AHEAD = 2


def ring_place(index, n):
    half = n // 2
    return jnp.where(index < half, index, n + half - 1 - index)


def kernel(
    n, wide, amap_ref, bmap_ref, owner_ref, a_ref, b_ref, out_ref,
    a_raw, b_raw, a_hi, a_lo, gathered, partial_c, half_in, half_sum, piece_in, panel,
    a_sem, b_sem, g_send, g_recv, x_send, x_recv, z_send, z_recv, p_send, p_recv, s_send, s_recv,
):
    rows, _, _, inner, side, _ = a_ref.shape
    chunks = b_ref.shape[3]
    hops = n // 2
    mates = wide // 2
    chunk_rows = rows * side
    half_rows = chunk_rows // 2
    piece = chunk_rows // wide

    blk, me = lax.axis_index("blk"), lax.axis_index("wide")
    place = ring_place(blk, n)
    right = ring_place(lax.rem(place + 1, n), n)
    left = ring_place(lax.rem(place + n - 1, n), n)
    core, chip = lax.rem(me, 2), me // 2
    partner = me + 1 - 2 * core
    mate = [None] + [2 * lax.rem(chip + d, mates) + core for d in range(1, mates)]
    my_half = pl.multiple_of(core * half_rows, 8)
    other_half = pl.multiple_of((1 - core) * half_rows, 8)
    my_place = core * half_rows + chip * piece
    my_row, my_start = my_place // side, pl.multiple_of(lax.rem(my_place, side), 8)

    def load_b(k):
        return pltpu.make_async_copy(b_ref.at[0, 0, :, k], b_raw.at[k], b_sem.at[k])

    load_a = pltpu.make_async_copy(a_ref, a_raw, a_sem)
    for k in range(chunks):
        load_b(k).start()
    load_a.start()

    barrier = pltpu.get_barrier_semaphore()
    for other in (left, right):
        pl.semaphore_signal(barrier, inc=1, device_id=(other, me), device_id_type=MESH)
    for other in [partner] + mate[1:]:
        pl.semaphore_signal(barrier, inc=1, device_id=(blk, other), device_id_type=MESH)

    def mask_b(k):
        load_b(k).wait()
        for t in range(inner):
            gathered[0, k, t] = b_raw[k, t] * bmap_ref[0, 0, t, k].astype(jnp.float32)

    mask_b(0)
    pl.semaphore_wait(barrier, 2 + mates)

    def hop(k, s, way):
        src = s - 1 if way == 0 else (n - s + 1) % n
        dst = s if way == 0 else n - s
        part = pl.ds(0, inner)
        if s == hops:
            part = pl.ds(0, inner // 2) if way == 0 else pl.ds(inner // 2, inner - inner // 2)
        return pltpu.make_async_remote_copy(
            src_ref=gathered.at[src, k, part],
            dst_ref=gathered.at[dst, k, part],
            send_sem=g_send.at[way, k, s - 1],
            recv_sem=g_recv.at[way, k, s - 1],
            device_id=(right if way == 0 else left, me),
            device_id_type=MESH,
        )

    def start_hop(k, s):
        for way in (0, 1):
            hop(k, s, way).start()

    def cross(k):
        return pltpu.make_async_remote_copy(
            src_ref=partial_c.at[k, pl.ds(other_half, half_rows)],
            dst_ref=half_in.at[k],
            send_sem=x_send.at[k],
            recv_sem=x_recv.at[k],
            device_id=(blk, partner),
            device_id_type=MESH,
        )

    def scatter(k, d):
        to = pl.multiple_of(lax.rem(chip + d, mates) * piece, 8)
        return pltpu.make_async_remote_copy(
            src_ref=half_sum.at[k, pl.ds(to, piece)],
            dst_ref=piece_in.at[k, d - 1],
            send_sem=z_send.at[k],
            recv_sem=z_recv.at[k],
            device_id=(blk, mate[d]),
            device_id_type=MESH,
        )

    def spread(k, d):
        return pltpu.make_async_remote_copy(
            src_ref=panel.at[k * rows + my_row, pl.ds(my_start, piece)],
            dst_ref=panel.at[k * rows + my_row, pl.ds(my_start, piece)],
            send_sem=p_send.at[k],
            recv_sem=p_recv.at[k],
            device_id=(blk, mate[d]),
            device_id_type=MESH,
        )

    def share(k):
        return pltpu.make_async_remote_copy(
            src_ref=panel.at[pl.ds(k * rows + core * (rows // 2), rows // 2)],
            dst_ref=panel.at[pl.ds(k * rows + core * (rows // 2), rows // 2)],
            send_sem=s_send.at[k],
            recv_sem=s_recv.at[k],
            device_id=(blk, partner),
            device_id_type=MESH,
        )

    def wait_pieces(k, sem):
        pltpu.make_async_copy(piece_in.at[k], piece_in.at[k], sem.at[k]).wait()

    def add_slot(k, d, base):
        right_part = gathered[d, k].reshape(inner * side, side)
        high = right_part.astype(jnp.bfloat16)
        low = (right_part - high.astype(jnp.float32)).astype(jnp.bfloat16)
        both = jnp.dot(
            a_hi[d], jnp.concatenate([high, low], axis=1), preferred_element_type=jnp.float32
        )
        rest = jnp.dot(a_lo[d], high, preferred_element_type=jnp.float32)
        partial_c[k] = base + (both[:, :side] + (both[:, side:] + rest))

    def compute(k, s):
        if s == 1:
            partial_c[k] = jnp.zeros((chunk_rows, side), jnp.float32)
        if s == hops:
            add_slot(k, hops, partial_c[k])
            return
        first, stride, many = (n - 1, 1, 3) if s == 1 else (s, n - 2 * s, 2)

        @pl.loop(0, many)
        def _(i):
            add_slot(k, lax.rem(first + i * stride, n), partial_c[k])

    for k in range(min(AHEAD, chunks)):
        if k:
            mask_b(k)
        start_hop(k, 1)

    load_a.wait()

    @pl.loop(0, n)
    def _(d):
        origin = ring_place(lax.rem(place + n - d, n), n)
        for r in range(rows):
            for t in range(inner):
                block = a_raw[r, origin, 0, t] * amap_ref[r, origin, 0, t].astype(jnp.float32)
                high = block.astype(jnp.bfloat16)
                at = (d, pl.ds(r * side, side), pl.ds(t * side, side))
                a_hi[at] = high
                a_lo[at] = (block - high.astype(jnp.float32)).astype(jnp.bfloat16)

    farthest = sorted(range(1, mates), key=lambda d: abs(2 * d - mates))
    here = lambda k: 0 <= k < chunks
    for turn in range(chunks + hops + 1):
        for s in range(1, hops):
            k = turn - (s - 1)
            if here(k):
                for way in (0, 1):
                    hop(k, s, way).wait_recv()
                start_hop(k, s + 1)
            if s == 1 and here(k + AHEAD):
                mask_b(k + AHEAD)
                start_hop(k + AHEAD, 1)
            if here(k):
                compute(k, s)
        k = turn - hops
        if here(k):
            wait_pieces(k, z_recv)
            total = half_sum[k, pl.ds(pl.multiple_of(chip * piece, 8), piece)]
            for d in range(1, mates):
                total = total + piece_in[k, d - 1]
            panel[k * rows + my_row, pl.ds(my_start, piece)] = total
            for d in farthest:
                spread(k, d).start()
        k = turn - (hops - 1)
        if here(k):
            for way in (0, 1):
                hop(k, hops, way).wait_recv()
            compute(k, hops)
            cross(k).start()
            cross(k).wait_recv()
            half_sum[k] = partial_c[k, pl.ds(my_half, half_rows)] + half_in[k]
            for d in farthest:
                scatter(k, d).start()
        k = turn - (hops + 1)
        if here(k):
            wait_pieces(k, p_recv)
            share(k).start()

    slots = out_ref.shape[2]
    count = jnp.int32(0)
    found = [jnp.int32(-1)] * slots
    for q in range(rows * chunks):
        mine = owner_ref[q // chunks, q % chunks] == me
        at = (q % chunks) * rows + q // chunks
        found = [jnp.where(mine & (count == s), at, f) for s, f in enumerate(found)]
        count = count + mine.astype(jnp.int32)

    for k in range(chunks):
        share(k).wait_recv()
    for s in range(slots):
        taken = (found[s] >= 0).astype(jnp.float32)
        out_ref[0, 0, s] = panel[jnp.maximum(found[s], 0)] * taken

    for k in range(chunks):
        for s in range(1, hops + 1):
            for way in (0, 1):
                hop(k, s, way).wait_send()
        cross(k).wait_send()
        wait_pieces(k, z_send)
        wait_pieces(k, p_send)
        share(k).wait_send()


def per_device(n, wide, a_blocks, a_map, b_blocks, b_map, owner_map):
    rows, _, _, inner, side, _ = a_blocks.shape
    chunks = b_blocks.shape[3]
    hops, mates = n // 2, wide // 2
    chunk_rows = rows * side
    slots = max(2, 2 * rows * chunks // wide)
    f32, bf16 = jnp.float32, jnp.bfloat16
    dma = pltpu.SemaphoreType.DMA
    flops = 3 * 2 * chunk_rows * n * inner * side * chunks * side
    return pl.pallas_call(
        functools.partial(kernel, n, wide),
        out_shape=jax.ShapeDtypeStruct((1, 1, slots, side, side), f32),
        in_specs=[pl.BlockSpec(memory_space=pltpu.SMEM)] * 3
        + [pl.BlockSpec(memory_space=pl.ANY)] * 2,
        out_specs=pl.BlockSpec(memory_space=pltpu.VMEM),
        scratch_shapes=[
            pltpu.VMEM(a_blocks.shape, f32),
            pltpu.VMEM((chunks, inner, side, side), f32),
            pltpu.VMEM((n, chunk_rows, inner * side), bf16),
            pltpu.VMEM((n, chunk_rows, inner * side), bf16),
            pltpu.VMEM((n, chunks, inner, side, side), f32),
            pltpu.VMEM((chunks, chunk_rows, side), f32),
            pltpu.VMEM((chunks, chunk_rows // 2, side), f32),
            pltpu.VMEM((chunks, chunk_rows // 2, side), f32),
            pltpu.VMEM((chunks, mates - 1, chunk_rows // wide, side), f32),
            pltpu.VMEM((chunks * rows, side, side), f32),
            dma,
            dma((chunks,)),
            dma((2, chunks, hops)),
            dma((2, chunks, hops)),
        ]
        + [dma((chunks,))] * 8,
        compiler_params=pltpu.CompilerParams(
            collective_id=0, has_side_effects=True, vmem_limit_bytes=56 * 2**20
        ),
        cost_estimate=pl.CostEstimate(
            flops=flops, bytes_accessed=8 * 2**20, transcendentals=0
        ),
    )(a_map, b_map, owner_map, a_blocks, b_blocks)


def solution(mesh):
    in_specs = (
        P("blk", None, "wide", None, None, None),
        P("blk", None, "wide", None),
        P("blk", "wide", None, None, None, None),
        P("blk", "wide", None, None),
        P("blk", None),
    )
    out_specs = P("blk", "wide", None, None, None)
    return jax.shard_map(
        functools.partial(per_device, mesh.shape["blk"], mesh.shape["wide"]),
        mesh=mesh, in_specs=in_specs, out_specs=out_specs, check_vma=False,
    )
```
